32 devices in a mesh: groups: 2 (over y), inner: 2 (over x), outer: 4 (over z), pair: 2 (over core).
Axes of the slice: x: 2, y: 2, z: 4, core: 2. Of those that a mesh axis runs over, the one named last changes fastest.
Arguments:
- tokens: bfloat16 [32, 128, 4096], P(('groups', 'inner', 'outer', 'pair')), parts along dimension 0, may hold values from -6 to 6
- queries: bfloat16 [32, 128, 2048], P(('groups', 'inner', 'outer', 'pair')), parts along dimension 0, may hold values from -54 to 54
- keys: bfloat16 [32, 128, 512], P(('groups', 'inner', 'outer', 'pair')), parts along dimension 0, may hold values from -18 to 18
- grad_out: bfloat16 [32, 128, 2048], P(('groups', 'inner', 'outer', 'pair')), parts along dimension 0, may hold values from -6 to 6
- segment_ids: int32 [32, 128], P(('groups', 'inner', 'outer', 'pair')), parts along dimension 0, may hold values from 0 to 7, never falling along the last dimension, each value on 1 to 32 neighbouring positions
- levels: bfloat16 [4096, 512], P('inner'), may hold values from -127 to 127
- scales: bfloat16 [32, 512], P('inner'), may hold values from 0.00010919571 to 0.00043678284
Outputs:
- attn_out: bfloat16 [32, 128, 2048], P(('groups', 'inner', 'outer', 'pair')), parts along dimension 0
- grad_tokens: bfloat16 [32, 128, 4096], P(('groups', 'inner', 'outer', 'pair')), parts along dimension 0
- grad_weight: float32 [8192, 512], P(('groups', 'inner', 'outer', 'pair')), parts along dimension 0
The draws below stay inside these ranges and needn't reach their ends.
There are 2 independent parts, one for each index of `groups`. The reference program is written for one: setup_inputs(seed, part) draws one part's arguments, and reference() takes and returns one part's arrays. A program takes and returns all parts, laid end to end along the dimension named above; an argument that names none is the same for every part. Nothing has to cross between parts.
Inputs may be any that keep to these rules, and one draw needn't show every extreme that they name: `segment_ids`: within a sequence segment numbers never fall, and each of the 8 segments spans 1 to 32 tokens.
All inputs are finite; a program needn't handle non-finite values.
Results may differ from the reference program's by a relative error of at most 0.0063.
Values may be sent and summed in bfloat16 or wider, within the bound.
A program may use at most 64 MiB of HBM per device.

```python
import math
import jax
import jax.numpy as jnp
import numpy as np
from jax import lax

D = 4096
HD = 128
KVH = 4
GROUP = 4
TOK_DEV = 128
QH = 16
SEQS = 16


def base_normals(key):
    key_query, key_key = jax.random.split(key)
    query_base = jnp.clip(jax.random.normal(key_query, (SEQS, TOK_DEV, KVH, GROUP, HD), jnp.float32), -6.0, 6.0)
    key_base = jnp.clip(jax.random.normal(key_key, (SEQS, TOK_DEV, KVH, HD), jnp.float32), -6.0, 6.0)
    return (query_base, key_base)


def draw_keys(key, part):
    query_base, key_base = base_normals(key)
    result = key_base
    return result.reshape(SEQS, TOK_DEV, KVH * HD).astype(jnp.bfloat16)


def draw_queries(key, part):
    query_base, key_base = base_normals(key)
    result = query_base
    return result.reshape(SEQS, TOK_DEV, KVH * GROUP * HD).astype(jnp.bfloat16)


def spiked(values, rng, source, target, parts, factor):
    def block_of(position):
        return (jnp.arange(values.shape[position]) // (values.shape[position] // parts)).reshape((-1,) + (1,) * (values.ndim - 1 - position))

    near = jax.random.permutation(rng, parts)[block_of(target)]
    second = (block_of(target) + parts // 2) % parts
    return jnp.where((block_of(source) == near) | (block_of(source) == second), factor * values, values)


def block_scale(rng, shape, cuts, low, high):
    def one(position, parts):
        draws = jax.random.uniform(jax.random.fold_in(jax.random.fold_in(rng, 6), position), (parts,), jnp.float32, low / len(cuts), high / len(cuts))
        return jnp.repeat(jnp.exp(draws), shape[position] // parts).reshape((-1,) + (1,) * (len(shape) - position - 1))

    factor_of = one(*cuts[0])
    for cut in cuts[1:]:
        factor_of = factor_of * one(*cut)
    return factor_of


def length_profile(count, total, bound, slope):
    loads = [(1 << 20) // math.isqrt(rank ** slope) + 1 for rank in range(2, count + 1)]
    surplus, given = total - bound - (count - 1), [1] * (count - 1)
    while surplus > 0:
        free = [i for i in range(count - 1) if given[i] < bound]
        mass, remaining = sum([loads[i] for i in free]), surplus
        for i in free:
            extra = min(bound - given[i], max(1, remaining * loads[i] // mass), surplus)
            given[i] = given[i] + extra
            surplus = surplus - extra
    return np.array([bound] + given)


def ragged(rng, number_of, total, most, slope):
    if number_of == 2:
        one = jax.random.randint(rng, (), max(1, total - most), min(most, total - 1) + 1)
        return jnp.stack([one, total - one])
    sizes = jnp.asarray(length_profile(number_of, total, most, slope), jnp.int32)
    couples = (number_of - 1) // 2
    donor, taker = sizes[1:1 + 2 * couples:2], sizes[2:2 + 2 * couples:2]
    slack = jnp.minimum(donor - 1, most - taker)
    moved = jax.random.randint(jax.random.fold_in(rng, 1), (couples,), 0, 1 << 20) % (slack + 1)
    sizes = sizes.at[1:1 + 2 * couples:2].set(donor - moved).at[2:2 + 2 * couples:2].set(taker + moved)
    return sizes[jax.random.permutation(jax.random.fold_in(rng, 2), number_of)]


def gaussian(own_key, extent, scale, bound, cuts=(), dtype=jnp.bfloat16):
    drawn = jax.random.normal(own_key, extent, jnp.float32) * scale
    if len(cuts) > 0:
        drawn = block_scale(own_key, extent, cuts, -0.22, 0.18) * drawn
    return jnp.clip(drawn, min=-bound, max=bound).astype(dtype)


def noise_with(stream_key, extent, scale, reach, cuts, heavy, dtype=jnp.bfloat16):
    values = scale * jax.random.normal(stream_key, extent, jnp.float32)
    if cuts:
        values = values * block_scale(stream_key, extent, cuts, -0.22, 0.18)
    return jnp.clip(spiked(values, jax.random.fold_in(stream_key, 3), *heavy), -reach, reach).astype(dtype)


def setup_inputs(seed: int = 0, part: int = 0) -> dict:
    arg_keys = jax.random.split(jax.random.key(seed), 8)
    own_keys = jax.random.split(jax.random.fold_in(arg_keys[7], part), 8)
    return {
        "tokens": noise_with(own_keys[0], (SEQS, TOK_DEV, D), 1.0, 6.0, ((0, 16),), (0, 2, 16, 2.0)),
        "queries": draw_queries(jax.random.fold_in(jax.random.fold_in(arg_keys[7], part), 71), part),
        "keys": draw_keys(jax.random.fold_in(jax.random.fold_in(arg_keys[7], part), 71), part),
        "grad_out": gaussian(own_keys[3], (SEQS, TOK_DEV, QH * HD), 1.0, 6.0, ((0, 16),)),
        "segment_ids": jax.vmap(lambda own: jnp.searchsorted(jnp.cumsum(ragged(own, 8, TOK_DEV, TOK_DEV // 4, 0)), jnp.arange(TOK_DEV), side="right"))(jax.random.split(own_keys[4], SEQS)).reshape((SEQS, TOK_DEV)).astype(jnp.int32),
        "levels": jnp.clip(jax.random.uniform(arg_keys[5], (D, KVH * HD), jnp.float32, -127.0, 127.0) * block_scale(arg_keys[5], (D, KVH * HD), ((0, 2),), -0.4, 0.0), -127.0, 127.0).astype(jnp.bfloat16),
        "scales": jnp.clip(jnp.exp(math.log(0.00043678284) - 1.3862944 * jax.random.uniform(arg_keys[6], (D // 128, KVH * HD), jnp.float32) ** block_scale(arg_keys[6], (D // 128, KVH * HD), ((0, 2),), -0.2, 0.2)), 0.00010919571, 0.00043678284).astype(jnp.bfloat16),
    }


def dequantize(levels, scales):
    blocks = levels.astype(jnp.float32).reshape(scales.shape[0], 128, levels.shape[1])
    scaled = blocks * scales.astype(jnp.float32)[:, None, :]
    return scaled.reshape(levels.shape).astype(jnp.bfloat16)

def attend(token_rows, query_rows, key_rows, cotangent, segments, weight):
    values = jnp.dot(token_rows, weight, preferred_element_type=jnp.float32).astype(jnp.bfloat16)
    query_f = query_rows.astype(jnp.float32).reshape(TOK_DEV, KVH, GROUP, HD)
    key_f = key_rows.astype(jnp.float32).reshape(TOK_DEV, KVH, HD)
    scores = jnp.einsum('ikgd,jkd->kgij', query_f, key_f, precision=lax.Precision.HIGHEST) / math.sqrt(HD)
    positions = jnp.arange(TOK_DEV)
    allowed = (positions[None, :] <= positions[:, None]) & (segments[:, None] == segments[None, :])
    scores = jnp.where(allowed, scores, jnp.float32(-1e+30))
    row_max = lax.optimization_barrier(jnp.max(scores, axis=-1, keepdims=True))
    expo = jnp.exp(scores - row_max)
    attention_p = (expo / lax.optimization_barrier(jnp.sum(expo, axis=-1, keepdims=True))).astype(jnp.bfloat16)
    p_float = attention_p.astype(jnp.float32)
    value_f = values.astype(jnp.float32).reshape(TOK_DEV, KVH, HD)
    output = jnp.einsum('kgij,jkd->ikgd', p_float, value_f, precision=lax.Precision.HIGHEST)
    output = output.reshape(TOK_DEV, KVH * GROUP * HD).astype(jnp.bfloat16)
    grad_f = cotangent.astype(jnp.float32).reshape(TOK_DEV, KVH, GROUP, HD)
    grad_values = jnp.einsum('kgij,ikgd->jkd', p_float, grad_f, precision=lax.Precision.HIGHEST)
    grad_values = grad_values.reshape(TOK_DEV, KVH * HD).astype(jnp.bfloat16)
    grad_rows = lax.dot_general(grad_values, weight, (((1,), (1,)), ((), ())), preferred_element_type=jnp.float32).astype(jnp.bfloat16)
    partial_value = lax.dot_general(token_rows, grad_values, (((0,), (0,)), ((), ())), preferred_element_type=jnp.float32).astype(jnp.bfloat16)
    return (output, grad_rows, partial_value)

def reference(tokens, queries, keys, grad_out, segment_ids, levels, scales):
    weight = dequantize(levels, scales)

    def advance(running, sequence):
        token_rows, query_rows, key_rows, cotangent, segments = sequence
        output, grad_rows, partial_value = attend(token_rows, query_rows, key_rows, cotangent, segments, weight)
        return (running + partial_value.astype(jnp.float32), (output, grad_rows))
    start_sum = jnp.zeros((D, KVH * HD), jnp.float32)
    grad_weight, (attn_out, grad_tokens) = lax.scan(advance, start_sum, (tokens, queries, keys, grad_out, segment_ids))
    return (attn_out, grad_tokens, grad_weight)
```

```python
import functools
import math

import jax
import jax.numpy as jnp
from jax import lax
from jax.experimental import pallas as pl
from jax.experimental.pallas import tpu as pltpu
from jax.sharding import PartitionSpec as P

HD = 128
KVH = 4
GROUP = 4
TILE = 512
MESH = pl.DeviceIdType.MESH


def dot(a, b, dims):
    return lax.dot_general(a, b, (dims, ((), ())), preferred_element_type=jnp.float32)


def kernel(
    inner, outer, splits,
    tokens, queries, keys, grad_out, segments, levels, scales,
    attn_out, grad_tokens, grad_weight,
    weight, probs, tok_all, gv_all, part, pair_send, pair_recv, z_send, z_recv, acc,
    tok_s, tok_r, gv_s, gv_r, w_s, w_r, pair_s, pair_r, z_s, z_r,
):
    g = lax.axis_index("groups")
    x = lax.axis_index("inner")
    z = lax.axis_index("outer")
    c = lax.axis_index("pair")
    length = tokens.shape[1]
    shard = levels.shape[0]
    quarter = shard // 4
    piece = quarter // splits
    kv = levels.shape[1]
    rows = grad_weight.shape[0]
    per_tile = TILE // (2 * rows)
    tiles = shard // TILE

    x_to = [lax.rem(x + k, inner) for k in range(inner)]
    x_from = [lax.rem(x + inner - k, inner) for k in range(inner)]
    z_to = [lax.rem(z + k, outer) for k in range(outer)]
    mate = {"pair": 1 - c}
    across = {"groups": 1 - g}

    barrier = pltpu.get_barrier_semaphore()
    peers = [{"inner": x_to[k]} for k in range(1, inner)]
    peers += [{"outer": z_to[k]} for k in range(1, outer)]
    peers += [mate, across]
    for peer in peers:
        pl.semaphore_signal(barrier, inc=1, device_id=peer, device_id_type=MESH)
    pl.semaphore_wait(barrier, len(peers))

    def remote(src, dst, send, recv, peer):
        return pltpu.make_async_remote_copy(
            src_ref=src, dst_ref=dst, send_sem=send, recv_sem=recv,
            device_id=peer, device_id_type=MESH,
        )

    def aligned(value, unit):
        return pl.multiple_of(value, unit)

    if per_tile == 1:
        order = sorted(range(1, outer), key=lambda k: -min(k, outer - k)) + [0]
        tile_at = [z_to[k] for k in order]
    else:
        order = list(range(1, outer)) + [0]
        tile_at = list(range(tiles))

    def tok_copy(k, j):
        col = aligned(x_to[k] * shard + tile_at[j] * TILE, TILE)
        to = aligned(tile_at[j] * TILE, TILE)
        return remote(
            tokens.at[0, :, pl.ds(col, TILE)], tok_all.at[x, :, pl.ds(to, TILE)],
            tok_s.at[k - 1, j], tok_r.at[k - 1, j], {"inner": x_to[k]},
        )

    def gv_copy(k):
        return remote(
            gv_all.at[x], gv_all.at[x], gv_s.at[k - 1], gv_r.at[k - 1], {"inner": x_to[k]}
        )

    def w_copy(kind, k, n):
        owner = x if kind == 0 else x_from[k]
        group = 1 - g if kind == 3 else g
        row = aligned((group * 2 + c) * quarter + n * piece, piece)
        block = weight.at[owner, pl.ds(row, piece), :]
        peer = ({"inner": x_to[k]}, mate, across, mate)[kind]
        return remote(block, block, w_s.at[kind, k - 1, n], w_r.at[kind, k - 1, n], peer)

    half = max(1, tiles // 2)
    for j in range(half):
        for k in range(1, inner):
            tok_copy(k, j).start()

    def dequantize(q):
        blocks = quarter // 128
        lev = levels[pl.ds(aligned(q * quarter, quarter), quarter), :].astype(jnp.float32)
        for q_static in range(4):
            @pl.when(q == q_static)
            def _():
                sc = scales[q_static * blocks:(q_static + 1) * blocks, :].astype(jnp.float32)
                out = lev.reshape(blocks, 128, kv) * sc[:, None, :]
                weight[x, q_static * quarter:(q_static + 1) * quarter, :] = (
                    out.reshape(quarter, kv).astype(jnp.bfloat16)
                )

    seg = jnp.broadcast_to(segments[...].astype(jnp.float32), (length, length))
    pos_i = lax.broadcasted_iota(jnp.int32, (length, length), 0)
    pos_j = lax.broadcasted_iota(jnp.int32, (length, length), 1)
    allowed = (pos_j <= pos_i) & (seg == seg.T)
    for h in range(KVH):
        base = h * GROUP * HD
        key = keys[0, :, h * HD:(h + 1) * HD]
        query = jnp.concatenate(
            [queries[0, :, base + i * HD:base + (i + 1) * HD] for i in range(GROUP)], axis=0
        )
        cot = jnp.concatenate(
            [grad_out[0, :, base + i * HD:base + (i + 1) * HD] for i in range(GROUP)], axis=0
        )
        scores = dot(query, key, ((1,), (1,))) / math.sqrt(HD)
        scores = scores.reshape(GROUP, length, length)
        scores = jnp.where(allowed[None], scores, jnp.float32(-1e30))
        expo = jnp.exp(scores - jnp.max(scores, axis=-1, keepdims=True))
        p = (expo / jnp.sum(expo, axis=-1, keepdims=True)).astype(jnp.bfloat16)
        p = p.reshape(GROUP * length, length)
        probs[h] = p
        gv_all[x, :, h * HD:(h + 1) * HD] = dot(p, cot, ((0,), (0,))).astype(jnp.bfloat16)

    for k in range(1, inner):
        gv_copy(k).start()
    for j in range(half, tiles):
        for k in range(1, inner):
            tok_copy(k, j).start()
    mine = g * 2 + c
    dequantize(mine)
    for n in range(splits):
        for k in range(1, inner):
            w_copy(0, k, n).start()
    for k in range(1, 4):
        dequantize(lax.rem(mine + k, 4))

    tok_all[x] = tokens[0, :, pl.ds(aligned(x * shard, shard), shard)]
    gv_own = gv_all[x]

    def products(owner, first, count):
        w = weight[owner, pl.ds(first, count), :]
        col = aligned(owner * shard + first, 128)
        acc[...] += dot(tokens[0, :, pl.ds(col, count)], w, ((1,), (0,)))
        grad_tokens[0, :, pl.ds(col, count)] = dot(gv_own, w, ((1,), (1,))).astype(jnp.bfloat16)

    acc[...] = jnp.zeros_like(acc)
    for q in range(4):
        products(x, q * quarter, quarter)

    for k in range(1, inner):
        gv_copy(k).wait_recv()
    gv = gv_all[...].reshape(inner * length, kv)

    def pair_copy(j):
        block = pl.ds(tile_at[j] * per_tile, per_tile)
        return remote(
            pair_send.at[block], pair_recv.at[block], pair_s.at[j], pair_r.at[j], mate
        )

    def z_copy(k):
        return remote(
            z_send.at[z_to[k]], z_recv.at[k - 1], z_s.at[k - 1], z_r.at[k - 1],
            {"outer": z_to[k]},
        )

    def tile_sum(j):
        for k in range(1, inner):
            tok_copy(k, j).wait_recv()
        col = aligned(tile_at[j] * TILE, TILE)
        tok = tok_all[:, :, pl.ds(col, TILE)].reshape(inner * length, TILE)
        total = dot(tok, gv, ((0,), (0,))).reshape(per_tile, 2, rows, kv)
        block = pl.ds(tile_at[j] * per_tile, per_tile)
        part[block] = total
        pair_send[block] = part[block, 1 - c].astype(jnp.bfloat16)
        pair_copy(j).start()

    def send_along(k):
        to = z_to[k]
        total = part[to, c] + pair_recv[to].astype(jnp.float32)
        if k == 0:
            part[to, c] = total
        else:
            z_send[to] = total.astype(jnp.bfloat16)
            z_copy(k).start()

    for j in range(tiles):
        tile_sum(j)
        if per_tile == 1 and j > 0:
            pair_copy(j - 1).wait_recv()
            send_along(order[j - 1])
    if per_tile == 1:
        pair_copy(tiles - 1).wait_recv()
        send_along(order[tiles - 1])
    else:
        for j in range(tiles):
            pair_copy(j).wait_recv()
        for k in order:
            send_along(k)

    for n in range(splits):
        for k in range(1, inner):
            w_copy(0, k, n).wait_recv()
            w_copy(2, k, n).start()
            w_copy(1, k, n).start()
            products(x_from[k], aligned(mine * quarter + n * piece, piece), piece)
    other = (1 - g) * 2 + c
    for n in range(splits):
        for k in range(1, inner):
            w_copy(2, k, n).wait_recv()
            w_copy(3, k, n).start()
            products(x_from[k], aligned(other * quarter + n * piece, piece), piece)
            w_copy(1, k, n).wait_recv()
            products(x_from[k], aligned((g * 2 + 1 - c) * quarter + n * piece, piece), piece)
    for n in range(splits):
        for k in range(1, inner):
            w_copy(3, k, n).wait_recv()
            products(x_from[k], aligned(((1 - g) * 2 + 1 - c) * quarter + n * piece, piece), piece)

    values = acc[...].astype(jnp.bfloat16)
    for h in range(KVH):
        out = dot(probs[h], values[:, h * HD:(h + 1) * HD], ((1,), (0,))).astype(jnp.bfloat16)
        for i in range(GROUP):
            col = (h * GROUP + i) * HD
            attn_out[0, :, col:col + HD] = out[i * length:(i + 1) * length]

    total = part[z, c]
    for k in order[:-1]:
        z_copy(k).wait_recv()
        total += z_recv[k - 1].astype(jnp.float32)
    grad_weight[...] = total

    for k in range(1, inner):
        gv_copy(k).wait_send()
        for j in range(tiles):
            tok_copy(k, j).wait_send()
        for n in range(splits):
            for kind in range(4):
                w_copy(kind, k, n).wait_send()
    for j in range(tiles):
        pair_copy(j).wait_send()
    for k in range(1, outer):
        z_copy(k).wait_send()


def shards(inner, outer, tokens, queries, keys, grad_out, segment_ids, levels, scales):
    length, width = tokens.shape[1:]
    shard, kv = levels.shape
    rows = shard // (2 * outer)
    quarter = shard // 4
    splits = max(1, quarter // 256)
    tiles = shard // TILE
    vmem = pl.BlockSpec(memory_space=pltpu.VMEM)
    bf16 = jnp.bfloat16
    dma = pltpu.SemaphoreType.DMA
    return pl.pallas_call(
        functools.partial(kernel, inner, outer, splits),
        out_shape=(
            jax.ShapeDtypeStruct(queries.shape, bf16),
            jax.ShapeDtypeStruct(tokens.shape, bf16),
            jax.ShapeDtypeStruct((rows, kv), jnp.float32),
        ),
        in_specs=[vmem] * 7,
        out_specs=(vmem,) * 3,
        scratch_shapes=[
            pltpu.VMEM((inner, shard, kv), bf16),
            pltpu.VMEM((KVH, GROUP * length, length), bf16),
            pltpu.VMEM((inner, length, shard), bf16),
            pltpu.VMEM((inner, length, kv), bf16),
            pltpu.VMEM((outer, 2, rows, kv), jnp.float32),
            pltpu.VMEM((outer, rows, kv), bf16),
            pltpu.VMEM((outer, rows, kv), bf16),
            pltpu.VMEM((outer, rows, kv), bf16),
            pltpu.VMEM((outer - 1, rows, kv), bf16),
            pltpu.VMEM((length, kv), jnp.float32),
            dma((inner - 1, tiles)), dma((inner - 1, tiles)),
            dma((inner - 1,)), dma((inner - 1,)),
            dma((4, inner - 1, splits)), dma((4, inner - 1, splits)),
            dma((tiles,)), dma((tiles,)),
            dma((outer - 1,)), dma((outer - 1,)),
        ],
        compiler_params=pltpu.CompilerParams(
            collective_id=0, has_side_effects=True, vmem_limit_bytes=48 * 1024 * 1024
        ),
    )(tokens, queries, keys, grad_out, segment_ids, levels, scales)


def solution(mesh):
    spread = ("groups", "inner", "outer", "pair")
    return jax.shard_map(
        functools.partial(shards, mesh.shape["inner"], mesh.shape["outer"]),
        mesh=mesh,
        in_specs=(
            P(spread, None, None),
            P(spread, None, None),
            P(spread, None, None),
            P(spread, None, None),
            P(spread, None),
            P("inner", None),
            P("inner", None),
        ),
        out_specs=(P(spread, None, None), P(spread, None, None), P(spread, None)),
        check_vma=False,
    )
```

```python
import functools
import math

import jax
import jax.numpy as jnp
from jax import lax
from jax.experimental import pallas as pl
from jax.experimental.pallas import tpu as pltpu
from jax.sharding import PartitionSpec as P

HD = 128
KVH = 4
GROUP = 4
TILE = 512
MESH = pl.DeviceIdType.MESH


def dot(a, b, dims):
    return lax.dot_general(a, b, (dims, ((), ())), preferred_element_type=jnp.float32)


def kernel(
    inner, outer, splits,
    tokens_hbm, queries_hbm, keys_hbm, grad_out_hbm, segments_hbm, levels_hbm, scales_hbm,
    attn_hbm, grad_tokens_hbm, grad_weight_hbm,
    tokens, queries, keys, grad_out, segments, levels, scales, in_sem,
    attn_out, grad_tokens, grad_weight, out_sem, piece_sem,
    weight, probs, tok_all, gv_all, part, pair_send, pair_recv, z_send, z_recv, acc,
    tok_s, tok_r, gv_s, gv_r, w_s, w_r, pair_s, pair_r, z_s, z_r,
):
    g = lax.axis_index("groups")
    x = lax.axis_index("inner")
    z = lax.axis_index("outer")
    c = lax.axis_index("pair")
    length = tokens_hbm.shape[1]
    shard = levels_hbm.shape[0]
    quarter = shard // 4
    piece = quarter // splits
    kv = levels_hbm.shape[1]
    rows = grad_weight_hbm.shape[0]
    per_tile = TILE // (2 * rows)
    tiles = shard // TILE

    x_to = [lax.rem(x + k, inner) for k in range(inner)]
    x_from = [lax.rem(x + inner - k, inner) for k in range(inner)]
    z_to = [lax.rem(z + k, outer) for k in range(outer)]
    mate = {"pair": 1 - c}
    across = {"groups": 1 - g}

    own = pl.ds(pl.multiple_of(x * shard, shard), shard)
    loads = [
        (queries_hbm, queries), (keys_hbm, keys), (segments_hbm, segments), (grad_out_hbm, grad_out),
        (levels_hbm, levels), (scales_hbm, scales), (tokens_hbm, tokens),
        (tokens_hbm.at[0, :, own], tok_all.at[x]),
    ]
    loads = [pltpu.make_async_copy(a, b, in_sem.at[i]) for i, (a, b) in enumerate(loads)]
    for load in loads:
        load.start()

    def piece_store(owner, row, index):
        cols = pl.ds(pl.multiple_of(owner * shard + row, piece), piece)
        return pltpu.make_async_copy(
            grad_tokens.at[0, :, cols], grad_tokens_hbm.at[0, :, cols], piece_sem.at[index]
        )

    own_store = pltpu.make_async_copy(
        grad_tokens.at[0, :, own], grad_tokens_hbm.at[0, :, own], out_sem.at[0]
    )
    attn_store = pltpu.make_async_copy(attn_out, attn_hbm, out_sem.at[1])
    weight_store = pltpu.make_async_copy(grad_weight, grad_weight_hbm, out_sem.at[2])

    barrier = pltpu.get_barrier_semaphore()
    peers = [{"inner": x_to[k]} for k in range(1, inner)]
    peers += [{"outer": z_to[k]} for k in range(1, outer)]
    peers += [mate, across]
    for peer in peers:
        pl.semaphore_signal(barrier, inc=1, device_id=peer, device_id_type=MESH)
    pl.semaphore_wait(barrier, len(peers))

    def remote(src, dst, send, recv, peer):
        return pltpu.make_async_remote_copy(
            src_ref=src, dst_ref=dst, send_sem=send, recv_sem=recv,
            device_id=peer, device_id_type=MESH,
        )

    def aligned(value, unit):
        return pl.multiple_of(value, unit)

    if per_tile == 1:
        order = sorted(range(1, outer), key=lambda k: -min(k, outer - k)) + [0]
        tile_at = [z_to[k] for k in order]
    else:
        order = list(range(1, outer)) + [0]
        tile_at = list(range(tiles))

    def tok_copy(k, j):
        col = aligned(x_to[k] * shard + tile_at[j] * TILE, TILE)
        to = aligned(tile_at[j] * TILE, TILE)
        return remote(
            tokens_hbm.at[0, :, pl.ds(col, TILE)], tok_all.at[x, :, pl.ds(to, TILE)],
            tok_s.at[k - 1, j], tok_r.at[k - 1, j], {"inner": x_to[k]},
        )

    def gv_copy(k):
        return remote(
            gv_all.at[x], gv_all.at[x], gv_s.at[k - 1], gv_r.at[k - 1], {"inner": x_to[k]}
        )

    def w_copy(kind, k, n):
        owner = x if kind == 0 else x_from[k]
        group = 1 - g if kind == 3 else g
        row = aligned((group * 2 + c) * quarter + n * piece, piece)
        block = weight.at[owner, pl.ds(row, piece), :]
        peer = ({"inner": x_to[k]}, mate, across, mate)[kind]
        return remote(block, block, w_s.at[kind, k - 1, n], w_r.at[kind, k - 1, n], peer)

    half = max(1, tiles // 2)
    for j in range(half):
        for k in range(1, inner):
            tok_copy(k, j).start()

    def dequantize(q):
        blocks = quarter // 128
        lev = levels[pl.ds(aligned(q * quarter, quarter), quarter), :].astype(jnp.float32)
        for q_static in range(4):
            @pl.when(q == q_static)
            def _():
                sc = scales[q_static * blocks:(q_static + 1) * blocks, :].astype(jnp.float32)
                out = lev.reshape(blocks, 128, kv) * sc[:, None, :]
                weight[x, q_static * quarter:(q_static + 1) * quarter, :] = (
                    out.reshape(quarter, kv).astype(jnp.bfloat16)
                )

    for load in loads[:4]:
        load.wait()
    seg = jnp.broadcast_to(segments[...].astype(jnp.float32), (length, length))
    pos_i = lax.broadcasted_iota(jnp.int32, (length, length), 0)
    pos_j = lax.broadcasted_iota(jnp.int32, (length, length), 1)
    allowed = (pos_j <= pos_i) & (seg == seg.T)
    for h in range(KVH):
        base = h * GROUP * HD
        key = keys[0, :, h * HD:(h + 1) * HD]
        query = jnp.concatenate(
            [queries[0, :, base + i * HD:base + (i + 1) * HD] for i in range(GROUP)], axis=0
        )
        cot = jnp.concatenate(
            [grad_out[0, :, base + i * HD:base + (i + 1) * HD] for i in range(GROUP)], axis=0
        )
        scores = dot(query, key, ((1,), (1,))) / math.sqrt(HD)
        scores = scores.reshape(GROUP, length, length)
        scores = jnp.where(allowed[None], scores, jnp.float32(-1e30))
        expo = jnp.exp(scores - jnp.max(scores, axis=-1, keepdims=True))
        p = (expo / jnp.sum(expo, axis=-1, keepdims=True)).astype(jnp.bfloat16)
        p = p.reshape(GROUP * length, length)
        probs[h] = p
        gv_all[x, :, h * HD:(h + 1) * HD] = dot(p, cot, ((0,), (0,))).astype(jnp.bfloat16)

    for k in range(1, inner):
        gv_copy(k).start()
    for j in range(half, tiles):
        for k in range(1, inner):
            tok_copy(k, j).start()
    mine = g * 2 + c
    for load in loads[4:]:
        load.wait()
    dequantize(mine)
    for n in range(splits):
        for k in range(1, inner):
            w_copy(0, k, n).start()
    for k in range(1, 4):
        dequantize(lax.rem(mine + k, 4))

    gv_own = gv_all[x]

    def products(owner, first, count):
        w = weight[owner, pl.ds(first, count), :]
        col = aligned(owner * shard + first, 128)
        acc[...] += dot(tokens[0, :, pl.ds(col, count)], w, ((1,), (0,)))
        grad_tokens[0, :, pl.ds(col, count)] = dot(gv_own, w, ((1,), (1,))).astype(jnp.bfloat16)

    acc[...] = jnp.zeros_like(acc)
    for q in range(4):
        products(x, q * quarter, quarter)
    own_store.start()

    for k in range(1, inner):
        gv_copy(k).wait_recv()
    gv = gv_all[...].reshape(inner * length, kv)

    def pair_copy(j):
        block = pl.ds(tile_at[j] * per_tile, per_tile)
        return remote(
            pair_send.at[block], pair_recv.at[block], pair_s.at[j], pair_r.at[j], mate
        )

    def z_copy(k):
        return remote(
            z_send.at[z_to[k]], z_recv.at[k - 1], z_s.at[k - 1], z_r.at[k - 1],
            {"outer": z_to[k]},
        )

    def tile_sum(j):
        for k in range(1, inner):
            tok_copy(k, j).wait_recv()
        col = aligned(tile_at[j] * TILE, TILE)
        tok = tok_all[:, :, pl.ds(col, TILE)].reshape(inner * length, TILE)
        total = dot(tok, gv, ((0,), (0,))).reshape(per_tile, 2, rows, kv)
        block = pl.ds(tile_at[j] * per_tile, per_tile)
        part[block] = total
        pair_send[block] = part[block, 1 - c].astype(jnp.bfloat16)
        pair_copy(j).start()

    def send_along(k):
        to = z_to[k]
        total = part[to, c] + pair_recv[to].astype(jnp.float32)
        if k == 0:
            part[to, c] = total
        else:
            z_send[to] = total.astype(jnp.bfloat16)
            z_copy(k).start()

    for j in range(tiles):
        tile_sum(j)
        if per_tile == 1 and j > 0:
            pair_copy(j - 1).wait_recv()
            send_along(order[j - 1])
    if per_tile == 1:
        pair_copy(tiles - 1).wait_recv()
        send_along(order[tiles - 1])
    else:
        for j in range(tiles):
            pair_copy(j).wait_recv()
        for k in order:
            send_along(k)

    stores = []

    def arrived(k, q, n):
        row = aligned(q * quarter + n * piece, piece)
        products(x_from[k], row, piece)
        store = piece_store(x_from[k], row, len(stores))
        store.start()
        stores.append(store)

    other = (1 - g) * 2 + c
    for n in range(splits):
        for k in range(1, inner):
            w_copy(0, k, n).wait_recv()
            w_copy(2, k, n).start()
            w_copy(1, k, n).start()
            arrived(k, mine, n)
    for n in range(splits):
        for k in range(1, inner):
            w_copy(2, k, n).wait_recv()
            w_copy(3, k, n).start()
            arrived(k, other, n)
            w_copy(1, k, n).wait_recv()
            arrived(k, g * 2 + 1 - c, n)
    for n in range(splits):
        for k in range(1, inner):
            w_copy(3, k, n).wait_recv()
            arrived(k, (1 - g) * 2 + 1 - c, n)

    values = acc[...].astype(jnp.bfloat16)
    for h in range(KVH):
        out = dot(probs[h], values[:, h * HD:(h + 1) * HD], ((1,), (0,))).astype(jnp.bfloat16)
        for i in range(GROUP):
            col = (h * GROUP + i) * HD
            attn_out[0, :, col:col + HD] = out[i * length:(i + 1) * length]

    attn_store.start()
    total = part[z, c]
    for k in order[:-1]:
        z_copy(k).wait_recv()
        total += z_recv[k - 1].astype(jnp.float32)
    grad_weight[...] = total
    weight_store.start()

    for k in range(1, inner):
        gv_copy(k).wait_send()
        for j in range(tiles):
            tok_copy(k, j).wait_send()
        for n in range(splits):
            for kind in range(4):
                w_copy(kind, k, n).wait_send()
    for j in range(tiles):
        pair_copy(j).wait_send()
    for k in range(1, outer):
        z_copy(k).wait_send()
    for store in [own_store, attn_store, weight_store] + stores:
        store.wait()


def shards(inner, outer, tokens, queries, keys, grad_out, segment_ids, levels, scales):
    length, width = tokens.shape[1:]
    shard, kv = levels.shape
    rows = shard // (2 * outer)
    quarter = shard // 4
    splits = max(1, quarter // 256)
    tiles = shard // TILE
    hbm = pl.BlockSpec(memory_space=pltpu.HBM)
    bf16 = jnp.bfloat16
    dma = pltpu.SemaphoreType.DMA
    results = pl.pallas_call(
        functools.partial(kernel, inner, outer, splits),
        out_shape=(
            jax.ShapeDtypeStruct(queries.shape, bf16),
            jax.ShapeDtypeStruct(tokens.shape, bf16),
            jax.ShapeDtypeStruct((rows, kv), jnp.float32),
        ),
        in_specs=[hbm] * 7,
        out_specs=(hbm,) * 3,
        scratch_shapes=[
            pltpu.VMEM(tokens.shape, bf16),
            pltpu.VMEM(queries.shape, bf16),
            pltpu.VMEM(keys.shape, bf16),
            pltpu.VMEM(grad_out.shape, bf16),
            pltpu.VMEM(segment_ids.shape, jnp.int32),
            pltpu.VMEM(levels.shape, bf16),
            pltpu.VMEM(scales.shape, bf16),
            dma((8,)),
            pltpu.VMEM(queries.shape, bf16),
            pltpu.VMEM(tokens.shape, bf16),
            pltpu.VMEM((rows, kv), jnp.float32),
            dma((3,)),
            dma(((inner - 1) * 4 * splits,)),
            pltpu.VMEM((inner, shard, kv), bf16),
            pltpu.VMEM((KVH, GROUP * length, length), bf16),
            pltpu.VMEM((inner, length, shard), bf16),
            pltpu.VMEM((inner, length, kv), bf16),
            pltpu.VMEM((outer, 2, rows, kv), jnp.float32),
            pltpu.VMEM((outer, rows, kv), bf16),
            pltpu.VMEM((outer, rows, kv), bf16),
            pltpu.VMEM((outer, rows, kv), bf16),
            pltpu.VMEM((outer - 1, rows, kv), bf16),
            pltpu.VMEM((length, kv), jnp.float32),
            dma((inner - 1, tiles)), dma((inner - 1, tiles)),
            dma((inner - 1,)), dma((inner - 1,)),
            dma((4, inner - 1, splits)), dma((4, inner - 1, splits)),
            dma((tiles,)), dma((tiles,)),
            dma((outer - 1,)), dma((outer - 1,)),
        ],
        compiler_params=pltpu.CompilerParams(
            collective_id=0, has_side_effects=True, vmem_limit_bytes=60 * 1024 * 1024
        ),
    )(tokens, queries, keys, grad_out, segment_ids, levels, scales)
    return results


def solution(mesh):
    spread = ("groups", "inner", "outer", "pair")
    return jax.shard_map(
        functools.partial(shards, mesh.shape["inner"], mesh.shape["outer"]),
        mesh=mesh,
        in_specs=(
            P(spread, None, None),
            P(spread, None, None),
            P(spread, None, None),
            P(spread, None, None),
            P(spread, None),
            P("inner", None),
            P("inner", None),
        ),
        out_specs=(P(spread, None, None), P(spread, None, None), P(spread, None)),
        check_vma=False,
    )
```

```python
import functools
import math

import jax
import jax.numpy as jnp
from jax import lax
from jax.experimental import pallas as pl
from jax.experimental.pallas import tpu as pltpu
from jax.sharding import PartitionSpec as P

HD = 128
KVH = 4
GROUP = 4
TILE = 512
SLICES = 2
MESH = pl.DeviceIdType.MESH


def dot(a, b, dims):
    return lax.dot_general(a, b, (dims, ((), ())), preferred_element_type=jnp.float32)


def kernel(
    inner, outer, splits,
    tokens_hbm, queries_hbm, keys_hbm, grad_out_hbm, segments_hbm, levels_hbm, scales_hbm,
    attn_hbm, grad_tokens_hbm, grad_weight_hbm,
    tokens, queries, keys, grad_out, segments, levels, scales, in_sem,
    attn_out, grad_tokens, grad_weight, out_sem, piece_sem,
    weight, probs, tok_all, gv_all, part, pair_send, pair_recv, z_send, z_recv, acc,
    tok_s, tok_r, gv_s, gv_r, w_s, w_r, pair_s, pair_r, z_s, z_r,
):
    g = lax.axis_index("groups")
    x = lax.axis_index("inner")
    z = lax.axis_index("outer")
    c = lax.axis_index("pair")
    length = tokens_hbm.shape[1]
    shard = levels_hbm.shape[0]
    quarter = shard // 4
    piece = quarter // splits
    kv = levels_hbm.shape[1]
    rows = grad_weight_hbm.shape[0]
    per_tile = TILE // (2 * rows)
    tiles = shard // TILE

    x_to = [lax.rem(x + k, inner) for k in range(inner)]
    x_from = [lax.rem(x + inner - k, inner) for k in range(inner)]
    z_to = [lax.rem(z + k, outer) for k in range(outer)]
    mate = {"pair": 1 - c}
    across = {"groups": 1 - g}

    own = pl.ds(pl.multiple_of(x * shard, shard), shard)
    loads = [
        (queries_hbm, queries), (keys_hbm, keys), (segments_hbm, segments), (grad_out_hbm, grad_out),
        (levels_hbm, levels), (scales_hbm, scales), (tokens_hbm, tokens),
        (tokens_hbm.at[0, :, own], tok_all.at[x]),
    ]
    loads = [pltpu.make_async_copy(a, b, in_sem.at[i]) for i, (a, b) in enumerate(loads)]
    for load in loads:
        load.start()

    def piece_store(owner, row, index):
        cols = pl.ds(pl.multiple_of(owner * shard + row, piece), piece)
        return pltpu.make_async_copy(
            grad_tokens.at[0, :, cols], grad_tokens_hbm.at[0, :, cols], piece_sem.at[index]
        )

    own_store = pltpu.make_async_copy(
        grad_tokens.at[0, :, own], grad_tokens_hbm.at[0, :, own], out_sem.at[0]
    )
    attn_store = pltpu.make_async_copy(attn_out, attn_hbm, out_sem.at[1])
    weight_store = pltpu.make_async_copy(grad_weight, grad_weight_hbm, out_sem.at[2])

    barrier = pltpu.get_barrier_semaphore()
    peers = [{"inner": x_to[k]} for k in range(1, inner)]
    peers += [{"outer": z_to[k]} for k in range(1, outer)]
    peers += [mate, across]
    for peer in peers:
        pl.semaphore_signal(barrier, inc=1, device_id=peer, device_id_type=MESH)
    pl.semaphore_wait(barrier, len(peers))

    def remote(src, dst, send, recv, peer):
        return pltpu.make_async_remote_copy(
            src_ref=src, dst_ref=dst, send_sem=send, recv_sem=recv,
            device_id=peer, device_id_type=MESH,
        )

    def aligned(value, unit):
        return pl.multiple_of(value, unit)

    if per_tile == 1:
        order = sorted(range(1, outer), key=lambda k: -min(k, outer - k)) + [0]
        tile_at = [z_to[k] for k in order]
    else:
        order = list(range(1, outer)) + [0]
        tile_at = list(range(tiles))

    def tok_copy(k, j):
        col = aligned(x_to[k] * shard + tile_at[j] * TILE, TILE)
        to = aligned(tile_at[j] * TILE, TILE)
        return remote(
            tokens_hbm.at[0, :, pl.ds(col, TILE)], tok_all.at[x, :, pl.ds(to, TILE)],
            tok_s.at[k - 1, j], tok_r.at[k - 1, j], {"inner": x_to[k]},
        )

    def gv_copy(k):
        return remote(
            gv_all.at[x], gv_all.at[x], gv_s.at[k - 1], gv_r.at[k - 1], {"inner": x_to[k]}
        )

    def w_copy(kind, k, n):
        owner = x if kind == 0 else x_from[k]
        group = 1 - g if kind == 3 else g
        row = aligned((group * 2 + c) * quarter + n * piece, piece)
        block = weight.at[owner, pl.ds(row, piece), :]
        peer = ({"inner": x_to[k]}, mate, across, mate)[kind]
        return remote(block, block, w_s.at[kind, k - 1, n], w_r.at[kind, k - 1, n], peer)

    half = min(1, tiles)
    for j in range(half):
        for k in range(1, inner):
            tok_copy(k, j).start()

    def dequantize(q):
        blocks = quarter // 128
        lev = levels[pl.ds(aligned(q * quarter, quarter), quarter), :].astype(jnp.float32)
        for q_static in range(4):
            @pl.when(q == q_static)
            def _():
                sc = scales[q_static * blocks:(q_static + 1) * blocks, :].astype(jnp.float32)
                out = lev.reshape(blocks, 128, kv) * sc[:, None, :]
                weight[x, q_static * quarter:(q_static + 1) * quarter, :] = (
                    out.reshape(quarter, kv).astype(jnp.bfloat16)
                )

    for load in loads[:4]:
        load.wait()
    seg = jnp.broadcast_to(segments[...].astype(jnp.float32), (length, length))
    pos_i = lax.broadcasted_iota(jnp.int32, (length, length), 0)
    pos_j = lax.broadcasted_iota(jnp.int32, (length, length), 1)
    allowed = (pos_j <= pos_i) & (seg == seg.T)
    for h in range(KVH):
        base = h * GROUP * HD
        key = keys[0, :, h * HD:(h + 1) * HD]
        query = jnp.concatenate(
            [queries[0, :, base + i * HD:base + (i + 1) * HD] for i in range(GROUP)], axis=0
        )
        cot = jnp.concatenate(
            [grad_out[0, :, base + i * HD:base + (i + 1) * HD] for i in range(GROUP)], axis=0
        )
        scores = dot(query, key, ((1,), (1,))) / math.sqrt(HD)
        scores = scores.reshape(GROUP, length, length)
        scores = jnp.where(allowed[None], scores, jnp.float32(-1e30))
        expo = jnp.exp(scores - jnp.max(scores, axis=-1, keepdims=True))
        p = (expo / jnp.sum(expo, axis=-1, keepdims=True)).astype(jnp.bfloat16)
        p = p.reshape(GROUP * length, length)
        probs[h] = p
        gv_all[x, :, h * HD:(h + 1) * HD] = dot(p, cot, ((0,), (0,))).astype(jnp.bfloat16)

    for k in range(1, inner):
        gv_copy(k).start()
    for j in range(half, tiles):
        for k in range(1, inner):
            tok_copy(k, j).start()
    mine = g * 2 + c
    for load in loads[4:]:
        load.wait()
    dequantize(mine)
    for n in range(splits):
        for k in range(1, inner):
            w_copy(0, k, n).start()
    gv_own = gv_all[x]

    def products(owner, first, count):
        w = weight[owner, pl.ds(first, count), :]
        col = aligned(owner * shard + first, 128)
        acc[...] += dot(tokens[0, :, pl.ds(col, count)], w, ((1,), (0,)))
        grad_tokens[0, :, pl.ds(col, count)] = dot(gv_own, w, ((1,), (1,))).astype(jnp.bfloat16)

    for k in range(1, inner):
        gv_copy(k).wait_recv()
    gv = gv_all[...].reshape(inner * length, kv)

    def pair_copy(j):
        block = pl.ds(tile_at[j] * per_tile, per_tile)
        return remote(
            pair_send.at[block], pair_recv.at[block], pair_s.at[j], pair_r.at[j], mate
        )

    def z_copy(k):
        return remote(
            z_send.at[z_to[k]], z_recv.at[k - 1], z_s.at[k - 1], z_r.at[k - 1],
            {"outer": z_to[k]},
        )

    def tile_sum(j):
        for k in range(1, inner):
            tok_copy(k, j).wait_recv()
        col = aligned(tile_at[j] * TILE, TILE)
        tok = tok_all[:, :, pl.ds(col, TILE)].reshape(inner * length, TILE)
        total = dot(tok, gv, ((0,), (0,))).reshape(per_tile, 2, rows, kv)
        block = pl.ds(tile_at[j] * per_tile, per_tile)
        part[block] = total
        pair_send[block] = part[block, 1 - c].astype(jnp.bfloat16)
        pair_copy(j).start()

    def send_along(k):
        to = z_to[k]
        total = part[to, c] + pair_recv[to].astype(jnp.float32)
        if k == 0:
            part[to, c] = total
        else:
            z_send[to] = total.astype(jnp.bfloat16)
            z_copy(k).start()

    for j in range(tiles):
        tile_sum(j)
        if per_tile == 1 and j > 0:
            pair_copy(j - 1).wait_recv()
            send_along(order[j - 1])
    if per_tile == 1:
        pair_copy(tiles - 1).wait_recv()
        send_along(order[tiles - 1])
    else:
        for j in range(tiles):
            pair_copy(j).wait_recv()
        for k in order:
            send_along(k)

    for k in range(1, 4):
        dequantize(lax.rem(mine + k, 4))

    acc[...] = jnp.zeros_like(acc)
    for q in range(4):
        products(x, q * quarter, quarter)
    own_store.start()

    stores = []

    def arrived(k, q, n):
        row = aligned(q * quarter + n * piece, piece)
        products(x_from[k], row, piece)
        store = piece_store(x_from[k], row, len(stores))
        store.start()
        stores.append(store)

    other = (1 - g) * 2 + c
    for n in range(splits):
        for k in range(1, inner):
            w_copy(0, k, n).wait_recv()
            w_copy(2, k, n).start()
            w_copy(1, k, n).start()
            arrived(k, mine, n)
    for n in range(splits):
        for k in range(1, inner):
            w_copy(2, k, n).wait_recv()
            w_copy(3, k, n).start()
            arrived(k, other, n)
            w_copy(1, k, n).wait_recv()
            arrived(k, g * 2 + 1 - c, n)
    for n in range(splits):
        for k in range(1, inner):
            w_copy(3, k, n).wait_recv()
            arrived(k, (1 - g) * 2 + 1 - c, n)

    values = acc[...].astype(jnp.bfloat16)
    for h in range(KVH):
        out = dot(probs[h], values[:, h * HD:(h + 1) * HD], ((1,), (0,))).astype(jnp.bfloat16)
        for i in range(GROUP):
            col = (h * GROUP + i) * HD
            attn_out[0, :, col:col + HD] = out[i * length:(i + 1) * length]

    attn_store.start()
    total = part[z, c]
    for k in order[:-1]:
        z_copy(k).wait_recv()
        total += z_recv[k - 1].astype(jnp.float32)
    grad_weight[...] = total
    weight_store.start()

    for k in range(1, inner):
        gv_copy(k).wait_send()
        for j in range(tiles):
            tok_copy(k, j).wait_send()
        for n in range(splits):
            for kind in range(4):
                w_copy(kind, k, n).wait_send()
    for j in range(tiles):
        pair_copy(j).wait_send()
    for k in range(1, outer):
        z_copy(k).wait_send()
    for store in [own_store, attn_store, weight_store] + stores:
        store.wait()


def store_kernel(copied, *refs):
    sources, targets, held, sem = refs[:3], refs[3:6], refs[6:9], refs[9]

    def copies(n):
        i, part = copied[n]
        width = held[i].shape[-1] // SLICES
        at = (slice(None),) * (len(held[i].shape) - 1) + (pl.ds(part * width, width),)
        return (
            pltpu.make_async_copy(sources[i].at[at], held[i].at[at], sem.at[0, n]),
            pltpu.make_async_copy(held[i].at[at], targets[i].at[at], sem.at[1, n]),
        )

    pairs = [copies(n) for n in range(len(copied))]
    for load, _ in pairs:
        load.start()
    for load, store in pairs:
        load.wait()
        store.start()
    for _, store in pairs:
        store.wait()


def shards(inner, outer, tokens, queries, keys, grad_out, segment_ids, levels, scales):
    length, width = tokens.shape[1:]
    shard, kv = levels.shape
    rows = shard // (2 * outer)
    quarter = shard // 4
    splits = max(1, quarter // 256)
    tiles = shard // TILE
    hbm = pl.BlockSpec(memory_space=pltpu.HBM)
    bf16 = jnp.bfloat16
    dma = pltpu.SemaphoreType.DMA
    results = pl.pallas_call(
        functools.partial(kernel, inner, outer, splits),
        out_shape=(
            jax.ShapeDtypeStruct(queries.shape, bf16),
            jax.ShapeDtypeStruct(tokens.shape, bf16),
            jax.ShapeDtypeStruct((rows, kv), jnp.float32),
        ),
        in_specs=[hbm] * 7,
        out_specs=(hbm,) * 3,
        scratch_shapes=[
            pltpu.VMEM(tokens.shape, bf16),
            pltpu.VMEM(queries.shape, bf16),
            pltpu.VMEM(keys.shape, bf16),
            pltpu.VMEM(grad_out.shape, bf16),
            pltpu.VMEM(segment_ids.shape, jnp.int32),
            pltpu.VMEM(levels.shape, bf16),
            pltpu.VMEM(scales.shape, bf16),
            dma((8,)),
            pltpu.VMEM(queries.shape, bf16),
            pltpu.VMEM(tokens.shape, bf16),
            pltpu.VMEM((rows, kv), jnp.float32),
            dma((3,)),
            dma(((inner - 1) * 4 * splits,)),
            pltpu.VMEM((inner, shard, kv), bf16),
            pltpu.VMEM((KVH, GROUP * length, length), bf16),
            pltpu.VMEM((inner, length, shard), bf16),
            pltpu.VMEM((inner, length, kv), bf16),
            pltpu.VMEM((outer, 2, rows, kv), jnp.float32),
            pltpu.VMEM((outer, rows, kv), bf16),
            pltpu.VMEM((outer, rows, kv), bf16),
            pltpu.VMEM((outer, rows, kv), bf16),
            pltpu.VMEM((outer - 1, rows, kv), bf16),
            pltpu.VMEM((length, kv), jnp.float32),
            dma((inner - 1, tiles)), dma((inner - 1, tiles)),
            dma((inner - 1,)), dma((inner - 1,)),
            dma((4, inner - 1, splits)), dma((4, inner - 1, splits)),
            dma((tiles,)), dma((tiles,)),
            dma((outer - 1,)), dma((outer - 1,)),
        ],
        compiler_params=pltpu.CompilerParams(
            collective_id=0, has_side_effects=True, vmem_limit_bytes=60 * 1024 * 1024
        ),
    )(tokens, queries, keys, grad_out, segment_ids, levels, scales)
    copied = [(i, part) for i, r in enumerate(results) for part in range(SLICES)]
    return pl.pallas_call(
        functools.partial(store_kernel, copied),
        out_shape=[jax.ShapeDtypeStruct(r.shape, r.dtype) for r in results],
        in_specs=[hbm] * 3,
        out_specs=[hbm] * 3,
        scratch_shapes=[pltpu.VMEM(r.shape, r.dtype) for r in results]
        + [dma((2, len(copied)))],
        compiler_params=pltpu.CompilerParams(vmem_limit_bytes=60 * 1024 * 1024),
    )(*results)


def solution(mesh):
    spread = ("groups", "inner", "outer", "pair")
    return jax.shard_map(
        functools.partial(shards, mesh.shape["inner"], mesh.shape["outer"]),
        mesh=mesh,
        in_specs=(
            P(spread, None, None),
            P(spread, None, None),
            P(spread, None, None),
            P(spread, None, None),
            P(spread, None),
            P("inner", None),
            P("inner", None),
        ),
        out_specs=(P(spread, None, None), P(spread, None, None), P(spread, None)),
        check_vma=False,
    )
```

```python
import functools
import math

import jax
import jax.numpy as jnp
from jax import lax
from jax.experimental import pallas as pl
from jax.experimental.pallas import tpu as pltpu
from jax.sharding import PartitionSpec as P

HD = 128
KVH = 4
GROUP = 4
TILE = 512
SLICES = 2
MESH = pl.DeviceIdType.MESH


def dot(a, b, dims):
    return lax.dot_general(a, b, (dims, ((), ())), preferred_element_type=jnp.float32)


def kernel(
    inner, outer, splits,
    tokens_hbm, queries_hbm, keys_hbm, grad_out_hbm, segments_hbm, levels_hbm, scales_hbm,
    attn_hbm, grad_tokens_hbm, grad_weight_hbm,
    tokens, queries, keys, grad_out, segments, levels, scales, in_sem,
    attn_out, grad_tokens, grad_weight, out_sem, piece_sem,
    weight, probs, tok_all, gv_all, part, pair_send, pair_recv, z_send, z_recv, acc,
    tok_s, tok_r, gv_s, gv_r, w_s, w_r, pair_s, pair_r, z_s, z_r,
):
    g = lax.axis_index("groups")
    x = lax.axis_index("inner")
    z = lax.axis_index("outer")
    c = lax.axis_index("pair")
    length = tokens_hbm.shape[1]
    shard = levels_hbm.shape[0]
    quarter = shard // 4
    piece = quarter // splits
    kv = levels_hbm.shape[1]
    rows = grad_weight_hbm.shape[0]
    per_tile = TILE // (2 * rows)
    tiles = shard // TILE

    x_to = [lax.rem(x + k, inner) for k in range(inner)]
    x_from = [lax.rem(x + inner - k, inner) for k in range(inner)]
    z_to = [lax.rem(z + k, outer) for k in range(outer)]
    mate = {"pair": 1 - c}
    across = {"groups": 1 - g}

    own = pl.ds(pl.multiple_of(x * shard, shard), shard)
    loads = [
        (queries_hbm, queries), (keys_hbm, keys), (segments_hbm, segments), (grad_out_hbm, grad_out),
        (levels_hbm, levels), (scales_hbm, scales), (tokens_hbm, tokens),
        (tokens_hbm.at[0, :, own], tok_all.at[x]),
    ]
    loads = [pltpu.make_async_copy(a, b, in_sem.at[i]) for i, (a, b) in enumerate(loads)]
    for load in loads:
        load.start()

    def piece_store(owner, row, index):
        cols = pl.ds(pl.multiple_of(owner * shard + row, piece), piece)
        return pltpu.make_async_copy(
            grad_tokens.at[0, :, cols], grad_tokens_hbm.at[0, :, cols], piece_sem.at[index]
        )

    own_store = pltpu.make_async_copy(
        grad_tokens.at[0, :, own], grad_tokens_hbm.at[0, :, own], out_sem.at[0]
    )
    attn_store = pltpu.make_async_copy(attn_out, attn_hbm, out_sem.at[1])
    weight_store = pltpu.make_async_copy(grad_weight, grad_weight_hbm, out_sem.at[2])

    barrier = pltpu.get_barrier_semaphore()
    peers = [{"inner": x_to[k]} for k in range(1, inner)]
    peers += [{"outer": z_to[k]} for k in range(1, outer)]
    peers += [mate, across]
    for peer in peers:
        pl.semaphore_signal(barrier, inc=1, device_id=peer, device_id_type=MESH)
    pl.semaphore_wait(barrier, len(peers))

    def remote(src, dst, send, recv, peer):
        return pltpu.make_async_remote_copy(
            src_ref=src, dst_ref=dst, send_sem=send, recv_sem=recv,
            device_id=peer, device_id_type=MESH,
        )

    def aligned(value, unit):
        return pl.multiple_of(value, unit)

    if per_tile == 1:
        order = sorted(range(1, outer), key=lambda k: -min(k, outer - k)) + [0]
        tile_at = [z_to[k] for k in order]
    else:
        order = list(range(1, outer)) + [0]
        tile_at = list(range(tiles))

    def tok_copy(k, j):
        col = aligned(x_to[k] * shard + tile_at[j] * TILE, TILE)
        to = aligned(tile_at[j] * TILE, TILE)
        return remote(
            tokens_hbm.at[0, :, pl.ds(col, TILE)], tok_all.at[x, :, pl.ds(to, TILE)],
            tok_s.at[k - 1, j], tok_r.at[k - 1, j], {"inner": x_to[k]},
        )

    def gv_copy(k):
        return remote(
            gv_all.at[x], gv_all.at[x], gv_s.at[k - 1], gv_r.at[k - 1], {"inner": x_to[k]}
        )

    def w_copy(kind, k, n):
        owner = x if kind == 0 else x_from[k]
        group = 1 - g if kind == 3 else g
        row = aligned((group * 2 + c) * quarter + n * piece, piece)
        block = weight.at[owner, pl.ds(row, piece), :]
        peer = ({"inner": x_to[k]}, mate, across, mate)[kind]
        return remote(block, block, w_s.at[kind, k - 1, n], w_r.at[kind, k - 1, n], peer)

    half = min(1, tiles)
    for j in range(half):
        for k in range(1, inner):
            tok_copy(k, j).start()

    def dequantize(q):
        blocks = quarter // 128
        lev = levels[pl.ds(aligned(q * quarter, quarter), quarter), :].astype(jnp.float32)
        for q_static in range(4):
            @pl.when(q == q_static)
            def _():
                sc = scales[q_static * blocks:(q_static + 1) * blocks, :].astype(jnp.float32)
                out = lev.reshape(blocks, 128, kv) * sc[:, None, :]
                weight[x, q_static * quarter:(q_static + 1) * quarter, :] = (
                    out.reshape(quarter, kv).astype(jnp.bfloat16)
                )

    for load in loads[:4]:
        load.wait()
    seg = jnp.broadcast_to(segments[...].astype(jnp.float32), (length, length))
    pos_i = lax.broadcasted_iota(jnp.int32, (length, length), 0)
    pos_j = lax.broadcasted_iota(jnp.int32, (length, length), 1)
    allowed = (pos_j <= pos_i) & (seg == seg.T)
    for h in range(KVH):
        base = h * GROUP * HD
        key = keys[0, :, h * HD:(h + 1) * HD]
        query = jnp.concatenate(
            [queries[0, :, base + i * HD:base + (i + 1) * HD] for i in range(GROUP)], axis=0
        )
        cot = jnp.concatenate(
            [grad_out[0, :, base + i * HD:base + (i + 1) * HD] for i in range(GROUP)], axis=0
        )
        scores = dot(query, key, ((1,), (1,))) / math.sqrt(HD)
        scores = scores.reshape(GROUP, length, length)
        scores = jnp.where(allowed[None], scores, jnp.float32(-1e30))
        expo = jnp.exp(scores - jnp.max(scores, axis=-1, keepdims=True))
        p = (expo / jnp.sum(expo, axis=-1, keepdims=True)).astype(jnp.bfloat16)
        p = p.reshape(GROUP * length, length)
        probs[h] = p
        gv_all[x, :, h * HD:(h + 1) * HD] = dot(p, cot, ((0,), (0,))).astype(jnp.bfloat16)

    for k in range(1, inner):
        gv_copy(k).start()
    for j in range(half, tiles):
        for k in range(1, inner):
            tok_copy(k, j).start()
    mine = g * 2 + c
    for load in loads[4:]:
        load.wait()
    dequantize(mine)
    for n in range(splits):
        for k in range(1, inner):
            w_copy(0, k, n).start()
    gv_own = gv_all[x]

    def products(owner, first, count):
        w = weight[owner, pl.ds(first, count), :]
        col = aligned(owner * shard + first, 128)
        acc[...] += dot(tokens[0, :, pl.ds(col, count)], w, ((1,), (0,)))
        grad_tokens[0, :, pl.ds(col, count)] = dot(gv_own, w, ((1,), (1,))).astype(jnp.bfloat16)

    for k in range(1, inner):
        gv_copy(k).wait_recv()
    gv = gv_all[...].reshape(inner * length, kv)

    def pair_copy(j):
        block = pl.ds(tile_at[j] * per_tile, per_tile)
        return remote(
            pair_send.at[block], pair_recv.at[block], pair_s.at[j], pair_r.at[j], mate
        )

    def z_copy(k):
        return remote(
            z_send.at[z_to[k]], z_recv.at[k - 1], z_s.at[k - 1], z_r.at[k - 1],
            {"outer": z_to[k]},
        )

    def tile_sum(j):
        for k in range(1, inner):
            tok_copy(k, j).wait_recv()
        col = aligned(tile_at[j] * TILE, TILE)
        tok = tok_all[:, :, pl.ds(col, TILE)].reshape(inner * length, TILE)
        total = dot(tok, gv, ((0,), (0,))).reshape(per_tile, 2, rows, kv)
        block = pl.ds(tile_at[j] * per_tile, per_tile)
        part[block] = total
        pair_send[block] = part[block, 1 - c].astype(jnp.bfloat16)
        pair_copy(j).start()

    def send_along(k):
        to = z_to[k]
        total = part[to, c] + pair_recv[to].astype(jnp.float32)
        if k == 0:
            part[to, c] = total
        else:
            z_send[to] = total.astype(jnp.bfloat16)
            z_copy(k).start()

    for j in range(tiles):
        tile_sum(j)
        if per_tile == 1 and j > 0:
            pair_copy(j - 1).wait_recv()
            send_along(order[j - 1])
    if per_tile == 1:
        pair_copy(tiles - 1).wait_recv()
        send_along(order[tiles - 1])
    else:
        for j in range(tiles):
            pair_copy(j).wait_recv()
        for k in order:
            send_along(k)

    stores = []

    def arrived(k, q, n):
        row = aligned(q * quarter + n * piece, piece)
        products(x_from[k], row, piece)
        store = piece_store(x_from[k], row, len(stores))
        store.start()
        stores.append(store)

    other = (1 - g) * 2 + c
    for n in range(splits):
        for k in range(1, inner):
            w_copy(0, k, n).wait_recv()
            w_copy(2, k, n).start()
            w_copy(1, k, n).start()
    for k in range(1, 4):
        dequantize(lax.rem(mine + k, 4))

    acc[...] = jnp.zeros_like(acc)
    for q in range(4):
        products(x, q * quarter, quarter)
    own_store.start()

    for n in range(splits):
        for k in range(1, inner):
            arrived(k, mine, n)
    for n in range(splits):
        for k in range(1, inner):
            w_copy(2, k, n).wait_recv()
            w_copy(3, k, n).start()
            arrived(k, other, n)
            w_copy(1, k, n).wait_recv()
            arrived(k, g * 2 + 1 - c, n)
    for n in range(splits):
        for k in range(1, inner):
            w_copy(3, k, n).wait_recv()
            arrived(k, (1 - g) * 2 + 1 - c, n)

    values = acc[...].astype(jnp.bfloat16)
    for h in range(KVH):
        out = dot(probs[h], values[:, h * HD:(h + 1) * HD], ((1,), (0,))).astype(jnp.bfloat16)
        for i in range(GROUP):
            col = (h * GROUP + i) * HD
            attn_out[0, :, col:col + HD] = out[i * length:(i + 1) * length]

    attn_store.start()
    total = part[z, c]
    for k in order[:-1]:
        z_copy(k).wait_recv()
        total += z_recv[k - 1].astype(jnp.float32)
    grad_weight[...] = total
    weight_store.start()

    for k in range(1, inner):
        gv_copy(k).wait_send()
        for j in range(tiles):
            tok_copy(k, j).wait_send()
        for n in range(splits):
            for kind in range(4):
                w_copy(kind, k, n).wait_send()
    for j in range(tiles):
        pair_copy(j).wait_send()
    for k in range(1, outer):
        z_copy(k).wait_send()
    for store in [own_store, attn_store, weight_store] + stores:
        store.wait()


def store_kernel(copied, *refs):
    sources, targets, held, sem = refs[:3], refs[3:6], refs[6:9], refs[9]

    def copies(n):
        i, part = copied[n]
        width = held[i].shape[-1] // SLICES
        at = (slice(None),) * (len(held[i].shape) - 1) + (pl.ds(part * width, width),)
        return (
            pltpu.make_async_copy(sources[i].at[at], held[i].at[at], sem.at[0, n]),
            pltpu.make_async_copy(held[i].at[at], targets[i].at[at], sem.at[1, n]),
        )

    pairs = [copies(n) for n in range(len(copied))]
    for load, _ in pairs:
        load.start()
    for load, store in pairs:
        load.wait()
        store.start()
    for _, store in pairs:
        store.wait()


def shards(inner, outer, tokens, queries, keys, grad_out, segment_ids, levels, scales):
    length, width = tokens.shape[1:]
    shard, kv = levels.shape
    rows = shard // (2 * outer)
    quarter = shard // 4
    splits = max(1, quarter // 256)
    tiles = shard // TILE
    hbm = pl.BlockSpec(memory_space=pltpu.HBM)
    bf16 = jnp.bfloat16
    dma = pltpu.SemaphoreType.DMA
    results = pl.pallas_call(
        functools.partial(kernel, inner, outer, splits),
        out_shape=(
            jax.ShapeDtypeStruct(queries.shape, bf16),
            jax.ShapeDtypeStruct(tokens.shape, bf16),
            jax.ShapeDtypeStruct((rows, kv), jnp.float32),
        ),
        in_specs=[hbm] * 7,
        out_specs=(hbm,) * 3,
        scratch_shapes=[
            pltpu.VMEM(tokens.shape, bf16),
            pltpu.VMEM(queries.shape, bf16),
            pltpu.VMEM(keys.shape, bf16),
            pltpu.VMEM(grad_out.shape, bf16),
            pltpu.VMEM(segment_ids.shape, jnp.int32),
            pltpu.VMEM(levels.shape, bf16),
            pltpu.VMEM(scales.shape, bf16),
            dma((8,)),
            pltpu.VMEM(queries.shape, bf16),
            pltpu.VMEM(tokens.shape, bf16),
            pltpu.VMEM((rows, kv), jnp.float32),
            dma((3,)),
            dma(((inner - 1) * 4 * splits,)),
            pltpu.VMEM((inner, shard, kv), bf16),
            pltpu.VMEM((KVH, GROUP * length, length), bf16),
            pltpu.VMEM((inner, length, shard), bf16),
            pltpu.VMEM((inner, length, kv), bf16),
            pltpu.VMEM((outer, 2, rows, kv), jnp.float32),
            pltpu.VMEM((outer, rows, kv), bf16),
            pltpu.VMEM((outer, rows, kv), bf16),
            pltpu.VMEM((outer, rows, kv), bf16),
            pltpu.VMEM((outer - 1, rows, kv), bf16),
            pltpu.VMEM((length, kv), jnp.float32),
            dma((inner - 1, tiles)), dma((inner - 1, tiles)),
            dma((inner - 1,)), dma((inner - 1,)),
            dma((4, inner - 1, splits)), dma((4, inner - 1, splits)),
            dma((tiles,)), dma((tiles,)),
            dma((outer - 1,)), dma((outer - 1,)),
        ],
        compiler_params=pltpu.CompilerParams(
            collective_id=0, has_side_effects=True, vmem_limit_bytes=60 * 1024 * 1024
        ),
    )(tokens, queries, keys, grad_out, segment_ids, levels, scales)
    copied = [(i, part) for i, r in enumerate(results) for part in range(SLICES)]
    return pl.pallas_call(
        functools.partial(store_kernel, copied),
        out_shape=[jax.ShapeDtypeStruct(r.shape, r.dtype) for r in results],
        in_specs=[hbm] * 3,
        out_specs=[hbm] * 3,
        scratch_shapes=[pltpu.VMEM(r.shape, r.dtype) for r in results]
        + [dma((2, len(copied)))],
        compiler_params=pltpu.CompilerParams(vmem_limit_bytes=60 * 1024 * 1024),
    )(*results)


def solution(mesh):
    spread = ("groups", "inner", "outer", "pair")
    return jax.shard_map(
        functools.partial(shards, mesh.shape["inner"], mesh.shape["outer"]),
        mesh=mesh,
        in_specs=(
            P(spread, None, None),
            P(spread, None, None),
            P(spread, None, None),
            P(spread, None, None),
            P(spread, None),
            P("inner", None),
            P("inner", None),
        ),
        out_specs=(P(spread, None, None), P(spread, None, None), P(spread, None)),
        check_vma=False,
    )
```
